32 devices in a mesh: gx: 8 (over z, core), gy: 4 (over y, x).
Axes of the slice: x: 2, y: 2, z: 4, core: 2. Of those that a mesh axis runs over, the one named last changes fastest.
Arguments:
- source_hat: float32 [2, 3, 256, 256, 256], P(None, None, 'gx', 'gy'), may hold values from -0.0014648438 to 0.0014648438
- particle_start: int32 [3, 65536], P(None, ('gx', 'gy')), may hold values from 0 to 255, as said below
- particle_offset: float32 [3, 65536], P(None, ('gx', 'gy')), may hold values from 0 to 1
- ghost_start: int32 [3, 3, 16384], P(None, None, ('gx', 'gy')), may hold values from 0 to 255, as said below
- ghost_offset: float32 [3, 3, 16384], P(None, None, ('gx', 'gy')), may hold values from 0 to 1, as said below
- ghost_slot: int32 [3, 16384], P(None, ('gx', 'gy')), may hold values from 0 to 2047, as said below
- counts: int32 [32, 4], P(('gx', 'gy')), may hold values from 0 to 2048, as said below
Outputs:
- velocity_far: float32 [3, 65536], P(None, ('gx', 'gy'))
- strain_far: float32 [5, 65536], P(None, ('gx', 'gy'))
The draws below stay inside these ranges and needn't reach their ends.
Inputs may be any that keep to these rules, and one draw needn't show every extreme that they name: `particle_start`: on device (a, b), a its gx index and b its gy index, every slot's x start lies in [b * 64, (b + 1) * 64) and its z start in [a * 32, (a + 1) * 32). `counts`: row of a device: its live own slots (the slots below this count are live), then the live entries of ghost groups 0, 1, 2 (the entries below each count are live); each ghost count is at most 512. `ghost_slot`: group 0 of device (a, b) lists particles of device (a, b - 1), group 1 of (a - 1, b), group 2 of (a - 1, b - 1), indices modulo the axis sizes; every entry is a slot index of that owner, below 2048; its live entries name distinct live slots of that owner, and they are exactly the owner's live particles whose support reaches the device's brick. `ghost_start`: A live ghost entry repeats the start of the owner's slot that ghost_slot names. `ghost_offset`: A live ghost entry repeats the offset of the owner's slot that ghost_slot names.
All inputs are finite; a program needn't handle non-finite values.
Results may differ from the reference program's by a relative error of at most 0.008.
Values sent between devices are 32-bit elements; how exact they have to be, the bound alone decides.
A program may use at most 256 MiB of HBM per device.

```python
import math
import jax
import jax.numpy as jnp
from jax import lax

GRID = 256
SUPPORT = 8
OWN = 2048
GHOST = 512
N_GX = 8
N_GY = 4


def particle_tables(key):
    device_count = N_GX * N_GY
    brick_x = GRID // N_GY
    brick_z = GRID // N_GX
    devices_all = jnp.arange(device_count, dtype=jnp.int32)
    busiest = jax.random.randint(jax.random.fold_in(key, 11), (), 0, device_count)
    live_counts = jax.random.randint(jax.random.fold_in(key, 12), (device_count,), OWN // 8, OWN // 2 + 1)
    live_counts = jnp.where(devices_all == busiest, OWN, live_counts).astype(jnp.int32)
    quotas = live_counts // 8
    score_keys = jax.random.split(jax.random.fold_in(key, 13), device_count)
    scores = jax.vmap(lambda score_key: jax.random.permutation(score_key, OWN))(score_keys).astype(jnp.int32)
    slot_ids = jnp.arange(OWN, dtype=jnp.int32)
    masked = jnp.where(slot_ids[None, :] < live_counts[:, None], scores, scores + OWN)
    by_rank = jnp.argsort(masked, axis=1, stable=True).astype(jnp.int32)
    rank_table = jnp.argsort(by_rank, axis=1, stable=True).astype(jnp.int32)
    quota_col = quotas[:, None]
    cross_x = (rank_table < quota_col) | (rank_table >= 2 * quota_col) & (rank_table < 3 * quota_col)
    cross_z = (rank_table >= quota_col) & (rank_table < 3 * quota_col)
    low_x = jnp.where(cross_x, brick_x - SUPPORT + 1, 0)
    high_x = jnp.where(cross_x, brick_x, brick_x - SUPPORT + 1)
    low_z = jnp.where(cross_z, brick_z - SUPPORT + 1, 0)
    high_z = jnp.where(cross_z, brick_z, brick_z - SUPPORT + 1)
    local_x = jax.random.randint(jax.random.fold_in(key, 14), (device_count, OWN), low_x, high_x)
    local_z = jax.random.randint(jax.random.fold_in(key, 15), (device_count, OWN), low_z, high_z)
    start_y = jax.random.randint(jax.random.fold_in(key, 16), (device_count, OWN), 0, GRID)
    block_z = devices_all // N_GY
    block_x = devices_all % N_GY
    start_x = block_x[:, None] * brick_x + local_x
    start_z = block_z[:, None] * brick_z + local_z
    starts = jnp.stack([start_x, start_y, start_z]).astype(jnp.int32)
    owners = jnp.stack([block_z * N_GY + (block_x - 1) % N_GY, (block_z - 1) % N_GX * N_GY + block_x, (block_z - 1) % N_GX * N_GY + (block_x - 1) % N_GY]).astype(jnp.int32)
    owner_quota = quotas[owners]
    entry_index = jnp.arange(GHOST, dtype=jnp.int32)[None, :]
    first_quota = owner_quota[0][:, None]
    rank_first = jnp.where(entry_index < first_quota, entry_index, entry_index + first_quota)
    rank_second = owner_quota[1][:, None] + entry_index
    rank_third = 2 * owner_quota[2][:, None] + entry_index
    rank_all = jnp.minimum(jnp.stack([rank_first, rank_second, rank_third]), OWN - 1)
    slot_table = jnp.take_along_axis(by_rank[owners], rank_all, axis=2).astype(jnp.int32)
    counts_table = jnp.stack([live_counts, 2 * owner_quota[0], 2 * owner_quota[1], owner_quota[2]], axis=1).astype(jnp.int32)
    return (starts, owners, slot_table, counts_table)


def particle_offsets(key):
    uniform_draw = jax.random.uniform(jax.random.fold_in(key, 21), (3, N_GX * N_GY, OWN), jnp.float32)
    return uniform_draw


def draw_particle_start(key, part):
    starts, owners, slot_table, counts_table = particle_tables(key)
    return starts.reshape(3, N_GX * N_GY * OWN)


def draw_particle_offset(key, part):
    return particle_offsets(key).reshape(3, N_GX * N_GY * OWN)


def draw_ghost_start(key, part):
    starts, owners, slot_table, counts_table = particle_tables(key)
    return starts[:, owners[:, :, None], slot_table].reshape(3, 3, N_GX * N_GY * GHOST)


def draw_ghost_offset(key, part):
    starts, owners, slot_table, counts_table = particle_tables(key)
    return particle_offsets(key)[:, owners[:, :, None], slot_table].reshape(3, 3, N_GX * N_GY * GHOST)


def draw_ghost_slot(key, part):
    starts, owners, slot_table, counts_table = particle_tables(key)
    return slot_table.reshape(3, N_GX * N_GY * GHOST)


def draw_counts(key, part):
    starts, owners, slot_table, counts_table = particle_tables(key)
    return counts_table


def level_of(key, extent, cuts, low, largest):
    level, own = 1.0, jax.random.fold_in(key, 6)
    for dim, parts in cuts:
        heights = jnp.exp(jax.random.uniform(jax.random.fold_in(own, dim), (parts,), jnp.float32, low / len(cuts), largest / len(cuts)))
        level = level * jnp.repeat(heights, extent[dim] // parts).reshape([-1 if axis == dim else 1 for axis in range(len(extent))])
    return level


def scatter_about(own_key, dims, scale, limit, shards=(), kind=jnp.bfloat16):
    drawn = scale * jax.random.normal(own_key, dims, jnp.float32)
    if shards:
        drawn = drawn * level_of(own_key, dims, shards, -0.22, 0.18)
    return jnp.clip(drawn, -limit, limit).astype(kind)


def setup_inputs(seed: int = 0) -> dict:
    arg_keys = jax.random.split(jax.random.key(seed), 8)
    return {
        "source_hat": scatter_about(arg_keys[0], (2, 3, GRID, GRID, GRID), (GRID * GRID * GRID) ** -0.5, 0.0014648438, ((2, 8), (3, 4)), jnp.float32),
        "particle_start": draw_particle_start(jax.random.fold_in(arg_keys[7], 71), 0),
        "particle_offset": draw_particle_offset(jax.random.fold_in(arg_keys[7], 71), 0),
        "ghost_start": draw_ghost_start(jax.random.fold_in(arg_keys[7], 71), 0),
        "ghost_offset": draw_ghost_offset(jax.random.fold_in(arg_keys[7], 71), 0),
        "ghost_slot": draw_ghost_slot(jax.random.fold_in(arg_keys[7], 71), 0),
        "counts": draw_counts(jax.random.fold_in(arg_keys[7], 71), 0),
    }


TWO_PI = 2.0 * math.pi


def signed_modes(count_modes):
    indices = jnp.arange(count_modes, dtype=jnp.int32)
    return jnp.where(indices < count_modes // 2, indices, indices - count_modes).astype(jnp.float32)


def spread_weight(distance, offset_value):
    shifted = distance - (SUPPORT // 2 - 1) - offset_value
    return jnp.exp(-5.6 * shifted * shifted / SUPPORT)


def grid_fields(source_hat):
    modes_all = signed_modes(GRID)
    mode_x = modes_all[:, None, None]
    mode_y = modes_all[None, :, None]
    mode_z = modes_all[None, None, :]
    square = jnp.maximum(mode_x * mode_x + mode_y * mode_y + mode_z * mode_z, 1.0)
    inner_product = source_hat[:, 0] * mode_x + source_hat[:, 1] * mode_y + source_hat[:, 2] * mode_z
    mode_list = (mode_x, mode_y, mode_z)
    velocity = [source_hat[:, comp_index] - mode_list[comp_index] * inner_product / square for comp_index in range(3)]
    complex_velocity = [part_pair[0] + 1j * part_pair[1] for part_pair in velocity]
    waves = [TWO_PI / GRID * mode_item for mode_item in mode_list]

    def derivative(comp_index, axis_index):
        return 1j * waves[axis_index] * complex_velocity[comp_index]

    spectra = [complex_velocity[0], complex_velocity[1], complex_velocity[2],
               derivative(0, 0), derivative(1, 1),
               0.5 * (derivative(0, 1) + derivative(1, 0)),
               0.5 * (derivative(0, 2) + derivative(2, 0)),
               0.5 * (derivative(1, 2) + derivative(2, 1))]
    return jnp.stack([jnp.real(jnp.fft.ifftn(spectrum, norm="forward")).astype(jnp.bfloat16) for spectrum in spectra])


def device_values(fields, device, start_rows, offset_rows, live_rows):
    brick_x = GRID // N_GY
    brick_z = GRID // N_GX
    block_z = device // N_GY
    block_x = device % N_GY
    steps_all = jnp.arange(SUPPORT, dtype=jnp.int32)
    cells_x = (start_rows[0][:, None] + steps_all[None, :]) % GRID
    cells_y = (start_rows[1][:, None] + steps_all[None, :]) % GRID
    cells_z = (start_rows[2][:, None] + steps_all[None, :]) % GRID
    inside_x = (cells_x // brick_x == block_x).astype(jnp.float32)
    inside_z = (cells_z // brick_z == block_z).astype(jnp.float32)
    distance = steps_all.astype(jnp.float32)[None, :]
    weight_x = spread_weight(distance, offset_rows[0][:, None]) * inside_x
    weight_y = spread_weight(distance, offset_rows[1][:, None])
    weight_z = spread_weight(distance, offset_rows[2][:, None]) * inside_z
    weight_plane = weight_x[:, :, None] * weight_z[:, None, :] * live_rows[:, None, None]
    weight_plane = lax.optimization_barrier(weight_plane.astype(jnp.bfloat16)).astype(jnp.float32)
    window = fields[:, cells_x[:, :, None, None], cells_y[:, None, :, None], cells_z[:, None, None, :]].astype(jnp.float32)
    return jnp.einsum("frijk,rik,rj->rf", window, weight_plane, weight_y)


def reference(source_hat, particle_start, particle_offset, ghost_start, ghost_offset, ghost_slot, counts):
    fields = lax.optimization_barrier(grid_fields(source_hat))
    device_count = N_GX * N_GY
    own_start = jnp.transpose(particle_start.reshape(3, device_count, OWN), (1, 0, 2))
    own_offset = jnp.transpose(particle_offset.reshape(3, device_count, OWN), (1, 0, 2))
    ghost_starts = jnp.transpose(ghost_start.reshape(3, 3, device_count, GHOST), (2, 0, 1, 3)).reshape(device_count, 3, 3 * GHOST)
    ghost_offsets = jnp.transpose(ghost_offset.reshape(3, 3, device_count, GHOST), (2, 0, 1, 3)).reshape(device_count, 3, 3 * GHOST)
    start_rows = jnp.concatenate([own_start, ghost_starts], axis=2)
    offset_rows = jnp.concatenate([own_offset, ghost_offsets], axis=2)
    own_live = jnp.arange(OWN, dtype=jnp.int32)[None, :] < counts[:, 0:1]
    ghost_live = jnp.arange(GHOST, dtype=jnp.int32)[None, None, :] < counts[:, 1:4, None]
    live_rows = jnp.concatenate([own_live, ghost_live.reshape(device_count, 3 * GHOST)], axis=1).astype(jnp.float32)
    devices_all = jnp.arange(device_count, dtype=jnp.int32)
    values = lax.map(lambda packed: device_values(fields, packed[0], packed[1], packed[2], packed[3]),
                     (devices_all, start_rows, offset_rows, live_rows))
    own_values = values[:, :OWN]
    ghost_values = values[:, OWN:].reshape(device_count, 3, GHOST, 8)
    block_z = devices_all // N_GY
    block_x = devices_all % N_GY
    owners = jnp.stack([block_z * N_GY + (block_x - 1) % N_GY,
                        ((block_z - 1) % N_GX) * N_GY + block_x,
                        ((block_z - 1) % N_GX) * N_GY + (block_x - 1) % N_GY], axis=1).astype(jnp.int32)
    slot_rows = jnp.transpose(ghost_slot.reshape(3, device_count, GHOST), (1, 0, 2))
    totals = own_values.at[owners[:, :, None], slot_rows].add(ghost_values)
    totals = jnp.transpose(totals, (2, 0, 1)).reshape(8, device_count * OWN)
    return totals[:3], totals[3:]
```

```python
import functools
import math

import jax
import jax.numpy as jnp
import numpy as np
from jax import lax
from jax.experimental import pallas as pl
from jax.experimental.pallas import tpu as pltpu
from jax.sharding import PartitionSpec as P

SUPPORT = 8
TWO_PI = 2.0 * math.pi
ROWS = 256
Z_GROUP = 8
VMEM_BYTES = 58 * 1024 * 1024
F32 = jnp.float32
BF16 = jnp.bfloat16


def signed(grid_size):
    index = np.arange(grid_size)
    return np.where(index < grid_size // 2, index, index - grid_size).astype(np.float64)


def dft_tables(grid_size):
    index = np.arange(grid_size)
    angle = (np.outer(index, index) % grid_size) * (TWO_PI / grid_size)
    cosine, sine = np.cos(angle), np.sin(angle)
    plain = np.stack([np.stack([cosine, sine], 1), np.stack([-sine, cosine], 1)])
    wave = (TWO_PI / grid_size * signed(grid_size))[None, :, None, None]
    slope = np.stack([np.stack([-sine, cosine], 1), np.stack([-cosine, -sine], 1)]) * wave
    return plain, slope


def two_parts(table):
    high = table.astype(np.float32).astype(jnp.bfloat16)
    low = (table - high.astype(np.float64)).astype(np.float32).astype(jnp.bfloat16)
    return jnp.asarray(high), jnp.asarray(low)


def split_value(value):
    high = value.astype(BF16)
    return high, (value - high.astype(F32)).astype(BF16)


def dot(left, right, dims):
    return lax.dot_general(left, right, (dims, ((), ())), preferred_element_type=F32)


def z_kernel(mx_ref, my_ref, mz_ref, s_ref, th_ref, tl_ref, dh_ref, dl_ref, out_ref, xh, xl):
    _, _, jb, ky, grid = s_ref.shape
    first = pl.program_id(0) * jb
    my = my_ref[...]
    mz = mz_ref[...]
    for jj in range(jb):
        mx = mx_ref[first + jj]
        inverse = 1.0 / jnp.maximum(mx * mx + my * my + mz * mz, 1.0)
        for r in range(2):
            s = [s_ref[r, c, jj] for c in range(3)]
            inner = (s[0] * mx + s[1] * my + s[2] * mz) * inverse
            for c, mode in enumerate((mx, my, mz)):
                high, low = split_value(s[c] - mode * inner)
                xh[c, jj * ky : (jj + 1) * ky, r * grid : (r + 1) * grid] = high
                xl[c, jj * ky : (jj + 1) * ky, r * grid : (r + 1) * grid] = low
    for f in range(5):
        c = f if f < 3 else f - 3
        high, low = (th_ref[...], tl_ref[...]) if f < 3 else (dh_ref[...], dl_ref[...])
        dims = ((1,), (1,))
        res = dot(high, xh[c], dims) + dot(low, xh[c], dims) + dot(high, xl[c], dims)
        parts = [
            jnp.concatenate(
                [res[:grid, jj * ky : (jj + 1) * ky], res[grid:, jj * ky : (jj + 1) * ky]], axis=1
            )
            for jj in range(jb)
        ]
        out_ref[:, f] = jnp.swapaxes(jnp.stack(parts), 0, 1)


def z_stage(source, mode_x, mode_y, mode_z):
    _, _, kx, ky, grid = source.shape
    jb = 8
    plain, slope = dft_tables(grid)

    def arranged(table):
        return two_parts(table.transpose(2, 3, 0, 1).reshape(2 * grid, 2 * grid))

    vmem = pl.BlockSpec(memory_space=pltpu.VMEM)
    return pl.pallas_call(
        z_kernel,
        grid=(kx // jb,),
        in_specs=[
            pl.BlockSpec(memory_space=pltpu.SMEM),
            vmem,
            vmem,
            pl.BlockSpec((2, 3, jb, ky, grid), lambda i: (0, 0, i, 0, 0)),
            vmem,
            vmem,
            vmem,
            vmem,
        ],
        out_specs=pl.BlockSpec((grid, 5, jb, 2 * ky), lambda i: (0, 0, i, 0)),
        out_shape=jax.ShapeDtypeStruct((grid, 5, kx, 2 * ky), F32),
        scratch_shapes=[
            pltpu.VMEM((3, jb * ky, 2 * grid), BF16),
            pltpu.VMEM((3, jb * ky, 2 * grid), BF16),
        ],
        compiler_params=pltpu.CompilerParams(vmem_limit_bytes=VMEM_BYTES),
        name="z_stage",
    )(mode_x, mode_y, mode_z, source, *arranged(plain), *arranged(slope))


def y_kernel(kx_ref, m_ref, th_ref, tl_ref, dh_ref, dl_ref, out_ref):
    pieces, zb, _, kx, width = m_ref.shape
    grid = th_ref.shape[1] // 2
    wave = kx_ref[...]

    def turned(value):
        return jnp.concatenate([-wave * value[:, grid:], wave * value[:, :grid]], axis=1)

    def one_plane(zi, carry):
        block = jnp.concatenate(
            [m_ref[b, zi].reshape(5 * kx, width) for b in range(pieces)], axis=1
        )
        high, low = split_value(block)
        dims = ((1,), (0,))
        y = (
            dot(high, th_ref[...], dims)
            + dot(high, tl_ref[...], dims)
            + dot(low, th_ref[...], dims)
        )
        high, low = high[: 3 * kx], low[: 3 * kx]
        d = (
            dot(high, dh_ref[...], dims)
            + dot(high, dl_ref[...], dims)
            + dot(low, dh_ref[...], dims)
        )
        v = [y[f * kx : (f + 1) * kx] for f in range(5)]
        dv = [d[f * kx : (f + 1) * kx] for f in range(3)]
        fields = [
            v[0],
            v[1],
            v[2],
            turned(v[0]),
            dv[1],
            0.5 * (dv[0] + turned(v[1])),
            0.5 * (v[3] + turned(v[2])),
            0.5 * (dv[2] + v[4]),
        ]
        both = jnp.concatenate(fields, axis=0).astype(BF16)
        lanes = pl.ds(pl.multiple_of(zi * grid, grid), grid)
        out_ref[0, : 8 * kx, lanes] = both[:, :grid]
        out_ref[0, 8 * kx :, lanes] = both[:, grid:]
        return carry

    lax.fori_loop(0, zb, one_plane, 0)


def y_stage(received, wave_x):
    pieces, z_count, _, kx, width = received.shape
    grid = pieces * width // 2
    plain, slope = dft_tables(grid)

    def arranged(table):
        table = table.reshape(2, pieces, width // 2, 2, grid).transpose(1, 0, 2, 3, 4)
        return two_parts(table.reshape(2 * grid, 2 * grid))

    vmem = pl.BlockSpec(memory_space=pltpu.VMEM)
    return pl.pallas_call(
        y_kernel,
        grid=(z_count // Z_GROUP,),
        in_specs=[
            vmem,
            pl.BlockSpec((pieces, Z_GROUP, 5, kx, width), lambda i: (0, i, 0, 0, 0)),
            vmem,
            vmem,
            vmem,
            vmem,
        ],
        out_specs=pl.BlockSpec((1, 16 * kx, Z_GROUP * grid), lambda i: (i, 0, 0)),
        out_shape=jax.ShapeDtypeStruct((z_count // Z_GROUP, 16 * kx, Z_GROUP * grid), BF16),
        compiler_params=pltpu.CompilerParams(vmem_limit_bytes=VMEM_BYTES),
        name="y_stage",
    )(wave_x, received, *arranged(plain), *arranged(slope))


def weights(cells, start, offset, grid):
    distance = cells - start
    distance = jnp.where(distance < 0, distance + grid, distance)
    shifted = distance - (SUPPORT // 2 - 1) - offset
    return jnp.where(distance < SUPPORT, jnp.exp(-5.6 * shifted * shifted / SUPPORT), 0.0)


def particle_kernel(live_ref, low_ref, high_ref, z0_ref, p_ref, table_ref, f_ref, out_ref, acc, wz_ref):
    block = pl.program_id(0)
    grid = table_ref.shape[1]
    groups = f_ref.shape[0]
    kx = table_ref.shape[0] // 2
    rows = p_ref.shape[1]
    live = live_ref[block]

    @pl.when(live <= 0)
    def _():
        out_ref[...] = jnp.zeros_like(out_ref)

    @pl.when(live > 0)
    def _():
        cells = lax.broadcasted_iota(jnp.int32, (grid, rows), 0).astype(F32)
        z_cells = lax.broadcasted_iota(jnp.int32, (groups * Z_GROUP, rows), 0) + z0_ref[0]
        wz = weights(z_cells.astype(F32), p_ref[2:3], p_ref[5:6], grid)
        lane = lax.broadcasted_iota(jnp.int32, (groups * Z_GROUP, rows), 1)
        wz_ref[...] = jnp.where(lane < live, wz, 0.0)
        wy = weights(cells, p_ref[1:2], p_ref[4:5], grid)
        acc[...] = jnp.zeros_like(acc)

        def one_group(g, carry):
            local = wz_ref[pl.ds(pl.multiple_of(g * Z_GROUP, Z_GROUP), Z_GROUP)]
            plane = jnp.concatenate(
                [(wy * local[z : z + 1]).astype(BF16) for z in range(Z_GROUP)], axis=0
            )
            acc[...] += dot(f_ref[g], plane, ((1,), (0,)))
            return carry

        lax.fori_loop(low_ref[block], high_ref[block], one_group, 0)
        wx = weights(cells, p_ref[0:1], p_ref[3:4], grid)
        wj = lax.dot_general(
            table_ref[...], wx, (((1,), (0,)), ((), ())),
            precision=lax.Precision.HIGHEST, preferred_element_type=F32,
        )
        product = acc[...].reshape(2, 8, kx, rows) * wj.reshape(2, 1, kx, rows)
        out_ref[...] = jnp.sum(product[0] + product[1], axis=1)


def particle_stage(live, low, high, z0, particles, table, fields):
    blocks = live.shape[0]
    vmem = pl.BlockSpec(memory_space=pltpu.VMEM)
    return pl.pallas_call(
        particle_kernel,
        grid_spec=pltpu.PrefetchScalarGridSpec(
            num_scalar_prefetch=4,
            grid=(blocks,),
            in_specs=[pl.BlockSpec((8, ROWS), lambda i, *_: (0, i)), vmem, vmem],
            out_specs=pl.BlockSpec((8, ROWS), lambda i, *_: (0, i)),
            scratch_shapes=[
                pltpu.VMEM((fields.shape[1], ROWS), F32),
                pltpu.VMEM((fields.shape[0] * Z_GROUP, ROWS), F32),
            ],
        ),
        out_shape=jax.ShapeDtypeStruct((8, blocks * ROWS), F32),
        compiler_params=pltpu.CompilerParams(vmem_limit_bytes=VMEM_BYTES),
        name="particle_stage",
    )(live, low, high, z0, particles, table, fields)


def per_device(
    source_hat, particle_start, particle_offset, ghost_start, ghost_offset, ghost_slot, counts
):
    _, _, kx, ky, grid = source_hat.shape
    n_gx = lax.axis_size("gx")
    n_gy = lax.axis_size("gy")
    a = lax.axis_index("gx")
    b = lax.axis_index("gy")
    ratio = n_gx // n_gy
    z_count = grid // n_gy
    brick_z = grid // n_gx
    own = particle_start.shape[1]
    ghost = ghost_start.shape[2]
    modes = jnp.asarray(signed(grid), F32)
    mode_x = lax.dynamic_slice(modes, (a * kx,), (kx,))
    mode_y = lax.dynamic_slice(modes, (b * ky,), (ky,))

    mine = jnp.concatenate(
        [
            jnp.concatenate([particle_start.astype(F32), ghost_start[:, 1].astype(F32)], axis=1),
            jnp.concatenate([particle_offset, ghost_offset[:, 1]], axis=1),
            jnp.concatenate([jnp.zeros((1, own), F32), ghost_slot[1:2].astype(F32)], axis=1),
            jnp.concatenate([counts.astype(F32), jnp.zeros((1, own + ghost - 4), F32)], axis=1),
        ]
    )
    every = lax.all_gather(mine, ("gx", "gy")).reshape(n_gx, n_gy, 8, own + ghost)
    near = lax.dynamic_slice(
        every, (ratio * b, 0, 0, 0), (ratio, n_gy, 8, own + ghost)
    ).reshape(ratio * n_gy, 8, own + ghost)
    lists = ratio * n_gy
    particles = jnp.concatenate(
        [
            jnp.moveaxis(near[:, :, :own], 1, 0).reshape(8, lists * own),
            jnp.moveaxis(near[:n_gy, :, own:], 1, 0).reshape(8, n_gy * ghost),
        ],
        axis=1,
    )
    near_counts = near[:, 7, :4].astype(jnp.int32)
    own_live = near_counts[:, :1] - jnp.arange(0, own, ROWS, dtype=jnp.int32)[None]
    ghost_live = near_counts[:n_gy, 2:3] - jnp.arange(0, ghost, ROWS, dtype=jnp.int32)[None]
    live = jnp.concatenate([own_live.reshape(-1), ghost_live.reshape(-1)])
    low, high = [], []
    for which in range(lists):
        first = which // n_gy * brick_z
        last = min(first + brick_z + SUPPORT - 1, z_count)
        low += [first // Z_GROUP] * (own // ROWS)
        high += [-(-last // Z_GROUP)] * (own // ROWS)
    low += [0] * (n_gy * ghost // ROWS)
    high += [-(-(SUPPORT - 1) // Z_GROUP)] * (n_gy * ghost // ROWS)
    low = jnp.asarray(low, jnp.int32)
    high = jnp.asarray(high, jnp.int32)

    along_z = z_stage(source_hat, mode_x, mode_y[:, None], modes[None, :])
    received = lax.all_to_all(along_z, "gy", split_axis=0, concat_axis=0, tiled=True)
    received = received.reshape(n_gy, z_count, 5, kx, 2 * ky)
    wave_x = jnp.broadcast_to((TWO_PI / grid * mode_x)[:, None], (kx, grid))
    fields = y_stage(received, wave_x)

    index = np.arange(grid)
    angle = (np.outer(index, index) % grid) * (TWO_PI / grid)
    full_table = jnp.asarray(np.stack([np.cos(angle), -np.sin(angle)]), F32)
    table = lax.dynamic_slice(full_table, (0, a * kx, 0), (2, kx, grid)).reshape(2 * kx, grid)
    z0 = (b * z_count).astype(jnp.int32).reshape(1)
    values = particle_stage(live, low, high, z0, particles, table, fields)

    own_values = values[:, : lists * own].reshape(8, ratio, n_gy * own)
    slots = near[:n_gy, 6, own:].astype(jnp.int32)
    slots = (slots + own * jnp.arange(n_gy, dtype=jnp.int32)[:, None]).reshape(-1)
    ghost_values = (
        jnp.zeros((8, n_gy * own), F32).at[:, slots].add(values[:, lists * own :])
    )
    spread = jnp.zeros((n_gx, 8, n_gy * own), F32)
    spread = lax.dynamic_update_slice(
        spread, jnp.moveaxis(own_values, 1, 0), (ratio * b, 0, 0)
    )
    spread = lax.dynamic_update_slice(
        spread, ghost_values[None], ((ratio * b + n_gx - 1) % n_gx, 0, 0)
    )
    total = lax.psum_scatter(spread, "gx", scatter_dimension=0, tiled=True)[0]
    total = lax.psum_scatter(total, "gy", scatter_dimension=1, tiled=True)
    return (total[:3], total[3:])


def solution(mesh):
    in_specs = (
        P(None, None, "gx", "gy", None),
        P(None, ("gx", "gy")),
        P(None, ("gx", "gy")),
        P(None, None, ("gx", "gy")),
        P(None, None, ("gx", "gy")),
        P(None, ("gx", "gy")),
        P(("gx", "gy"), None),
    )
    out_specs = (P(None, ("gx", "gy")), P(None, ("gx", "gy")))
    return jax.shard_map(
        per_device, mesh=mesh, in_specs=in_specs, out_specs=out_specs, check_vma=False
    )
```

```python
import functools
import math

import jax
import jax.numpy as jnp
import numpy as np
from jax import lax
from jax.experimental import pallas as pl
from jax.experimental.pallas import tpu as pltpu
from jax.sharding import PartitionSpec as P

SUPPORT = 8
TWO_PI = 2.0 * math.pi
ROWS = 256
Z_GROUP = 8
MODE_CHUNK = 16
VMEM_BYTES = 58 * 1024 * 1024
F32 = jnp.float32
BF16 = jnp.bfloat16


def signed(grid_size):
    index = np.arange(grid_size)
    return np.where(index < grid_size // 2, index, index - grid_size).astype(np.float64)


def dft_tables(grid_size):
    index = np.arange(grid_size)
    angle = (np.outer(index, index) % grid_size) * (TWO_PI / grid_size)
    cosine, sine = np.cos(angle), np.sin(angle)
    plain = np.stack([np.stack([cosine, sine], 1), np.stack([-sine, cosine], 1)])
    wave = (TWO_PI / grid_size * signed(grid_size))[None, :, None, None]
    slope = np.stack([np.stack([-sine, cosine], 1), np.stack([-cosine, -sine], 1)]) * wave
    return plain, slope


def two_parts(table):
    high = table.astype(np.float32).astype(jnp.bfloat16)
    low = (table - high.astype(np.float64)).astype(np.float32).astype(jnp.bfloat16)
    return jnp.asarray(high), jnp.asarray(low)


def split_value(value):
    high = value.astype(BF16)
    return high, (value - high.astype(F32)).astype(BF16)


def exact_dot(left, right_high, right_low):
    high, low = split_value(left)
    dims = ((1,), (0,))
    return dot(high, right_high, dims) + dot(high, right_low, dims) + dot(low, right_high, dims)


def dot(left, right, dims):
    return lax.dot_general(left, right, (dims, ((), ())), preferred_element_type=F32)


def z_kernel(mx_ref, my_ref, mz_ref, s_ref, th_ref, tl_ref, dh_ref, dl_ref, out_ref, xh, xl):
    _, _, jb, ky, grid = s_ref.shape
    first = pl.program_id(0) * jb
    my = my_ref[...]
    mz = mz_ref[...]
    for jj in range(jb):
        mx = mx_ref[first + jj]
        inverse = 1.0 / jnp.maximum(mx * mx + my * my + mz * mz, 1.0)
        for r in range(2):
            s = [s_ref[r, c, jj] for c in range(3)]
            inner = (s[0] * mx + s[1] * my + s[2] * mz) * inverse
            for c, mode in enumerate((mx, my, mz)):
                high, low = split_value(s[c] - mode * inner)
                xh[c, jj * ky : (jj + 1) * ky, r * grid : (r + 1) * grid] = high
                xl[c, jj * ky : (jj + 1) * ky, r * grid : (r + 1) * grid] = low
    for f in range(5):
        c = f if f < 3 else f - 3
        high, low = (th_ref[...], tl_ref[...]) if f < 3 else (dh_ref[...], dl_ref[...])
        dims = ((1,), (1,))
        res = dot(high, xh[c], dims) + dot(low, xh[c], dims) + dot(high, xl[c], dims)
        parts = [
            jnp.concatenate(
                [res[:grid, jj * ky : (jj + 1) * ky], res[grid:, jj * ky : (jj + 1) * ky]], axis=1
            )
            for jj in range(jb)
        ]
        out_ref[:, f] = jnp.swapaxes(jnp.stack(parts), 0, 1)


def cost(flops, nbytes):
    return pl.CostEstimate(flops=flops, bytes_accessed=nbytes, transcendentals=0)


def z_stage(source, mode_x, mode_y, mode_z, chunk, kx):
    _, _, _, ky, grid = source.shape
    jb = 8
    skip = chunk * kx // jb
    plain, slope = dft_tables(grid)

    def arranged(table):
        return two_parts(table.transpose(2, 3, 0, 1).reshape(2 * grid, 2 * grid))

    vmem = pl.BlockSpec(memory_space=pltpu.VMEM)
    return pl.pallas_call(
        z_kernel,
        grid=(kx // jb,),
        in_specs=[
            pl.BlockSpec(memory_space=pltpu.SMEM),
            vmem,
            vmem,
            pl.BlockSpec((2, 3, jb, ky, grid), lambda i: (0, 0, i + skip, 0, 0)),
            vmem,
            vmem,
            vmem,
            vmem,
        ],
        out_specs=pl.BlockSpec((grid, 5, jb, 2 * ky), lambda i: (0, 0, i, 0)),
        out_shape=jax.ShapeDtypeStruct((grid, 5, kx, 2 * ky), F32),
        scratch_shapes=[
            pltpu.VMEM((3, jb * ky, 2 * grid), BF16),
            pltpu.VMEM((3, jb * ky, 2 * grid), BF16),
        ],
        compiler_params=pltpu.CompilerParams(vmem_limit_bytes=VMEM_BYTES),
        cost_estimate=cost(3 * 5 * kx * ky * 8 * grid * grid, 4 * 16 * kx * ky * grid),
        name=f"z_stage_{chunk}",
    )(mode_x, mode_y, mode_z, source, *arranged(plain), *arranged(slope))


def y_kernel(kx_ref, m_ref, th_ref, tl_ref, dh_ref, dl_ref, *rest):
    out_ref = rest[-1]
    pieces, zb, _, kx, width = m_ref.shape
    grid = th_ref.shape[1] // 2
    wave = kx_ref[...]

    def turned(value):
        return jnp.concatenate([-wave * value[:, grid:], wave * value[:, :grid]], axis=1)

    block = jnp.concatenate(
        [m_ref[b].reshape(zb * 5 * kx, width) for b in range(pieces)], axis=1
    )
    components = jnp.concatenate(
        [block[z * 5 * kx : (z * 5 + 3) * kx] for z in range(zb)], axis=0
    )
    y = exact_dot(block, th_ref[...], tl_ref[...])
    d = exact_dot(components, dh_ref[...], dl_ref[...])
    for z in range(zb):
        v = [y[(z * 5 + f) * kx : (z * 5 + f + 1) * kx] for f in range(5)]
        dv = [d[(z * 3 + f) * kx : (z * 3 + f + 1) * kx] for f in range(3)]
        fields = [
            v[0],
            v[1],
            v[2],
            turned(v[0]),
            dv[1],
            0.5 * (dv[0] + turned(v[1])),
            0.5 * (v[3] + turned(v[2])),
            0.5 * (dv[2] + v[4]),
        ]
        both = jnp.concatenate(fields, axis=0).astype(BF16)
        out_ref[0, : 8 * kx, z * grid : (z + 1) * grid] = both[:, :grid]
        out_ref[0, 8 * kx :, z * grid : (z + 1) * grid] = both[:, grid:]


def y_stage(received, wave_x, chunk, after):
    pieces, z_count, _, kx, width = received.shape
    grid = pieces * width // 2
    plain, slope = dft_tables(grid)

    def arranged(table):
        table = table.reshape(2, pieces, width // 2, 2, grid).transpose(1, 0, 2, 3, 4)
        return two_parts(table.reshape(2 * grid, 2 * grid))

    vmem = pl.BlockSpec(memory_space=pltpu.VMEM)
    return pl.pallas_call(
        y_kernel,
        grid=(z_count // Z_GROUP,),
        in_specs=[
            vmem,
            pl.BlockSpec((pieces, Z_GROUP, 5, kx, width), lambda i: (0, i, 0, 0, 0)),
            vmem,
            vmem,
            vmem,
            vmem,
        ]
        + [pl.BlockSpec(memory_space=pl.ANY)] * len(after),
        out_specs=pl.BlockSpec((1, 16 * kx, Z_GROUP * grid), lambda i: (i, 0, 0)),
        out_shape=jax.ShapeDtypeStruct((z_count // Z_GROUP, 16 * kx, Z_GROUP * grid), BF16),
        compiler_params=pltpu.CompilerParams(vmem_limit_bytes=VMEM_BYTES),
        cost_estimate=cost(3 * 8 * 8 * kx * z_count * grid * grid, 72 * kx * z_count * grid),
        name=f"y_stage_{chunk}",
    )(wave_x, received, *arranged(plain), *arranged(slope), *after)


def follow(piece, earlier):
    any_space = pl.BlockSpec(memory_space=pl.ANY)
    return pl.pallas_call(
        lambda *refs: None,
        in_specs=[any_space, any_space],
        out_specs=any_space,
        out_shape=jax.ShapeDtypeStruct(piece.shape, piece.dtype),
        input_output_aliases={0: 0},
        compiler_params=pltpu.CompilerParams(vmem_limit_bytes=VMEM_BYTES),
        name="follow",
    )(piece, earlier)


def ghost_kernel(v_ref, p_ref, out_ref):
    own = out_ref.shape[2]
    ghost = v_ref.shape[1]
    slots = lax.broadcasted_iota(jnp.int32, (own, ghost), 0).astype(F32)
    hit = jnp.where(slots == p_ref[6:7], 1.0, 0.0).astype(BF16)
    value = v_ref[...]
    first, rest = split_value(value)
    rest = value - first.astype(F32)
    second, _ = split_value(rest)
    third = (rest - second.astype(F32)).astype(BF16)
    dims = ((1,), (1,))
    out_ref[0] = dot(first, hit, dims) + dot(second, hit, dims) + dot(third, hit, dims)


def ghost_stage(values, particles, own, ghost, lists, skip):
    block = pl.BlockSpec((8, ghost), lambda i: (0, i + skip // ghost))
    return pl.pallas_call(
        ghost_kernel,
        grid=(lists,),
        in_specs=[block, block],
        out_specs=pl.BlockSpec((1, 8, own), lambda i: (i, 0, 0)),
        out_shape=jax.ShapeDtypeStruct((lists, 8, own), F32),
        compiler_params=pltpu.CompilerParams(vmem_limit_bytes=VMEM_BYTES),
        name="ghost_stage",
    )(values, particles)


def weights(cells, start, offset, grid):
    distance = cells - start
    distance = jnp.where(distance < 0, distance + grid, distance)
    shifted = distance - (SUPPORT // 2 - 1) - offset
    return jnp.where(distance < SUPPORT, jnp.exp(-5.6 * shifted * shifted / SUPPORT), 0.0)


def particle_kernel(
    live_ref, low_ref, high_ref, z0_ref, p_ref, table_ref, f_ref, *rest
):
    *earlier, out_ref, acc, wz_ref = rest
    block = pl.program_id(0)
    grid = table_ref.shape[1]
    groups = f_ref.shape[0]
    kx = table_ref.shape[0] // 2
    rows = p_ref.shape[1]
    live = live_ref[block]

    @pl.when(live <= 0)
    def _():
        out_ref[...] = jnp.zeros_like(out_ref)

    @pl.when(live > 0)
    def _():
        cells = lax.broadcasted_iota(jnp.int32, (grid, rows), 0).astype(F32)
        z_cells = lax.broadcasted_iota(jnp.int32, (groups * Z_GROUP, rows), 0) + z0_ref[0]
        wz = weights(z_cells.astype(F32), p_ref[2:3], p_ref[5:6], grid)
        lane = lax.broadcasted_iota(jnp.int32, (groups * Z_GROUP, rows), 1)
        wz_ref[...] = jnp.where(lane < live, wz, 0.0)
        wy = weights(cells, p_ref[1:2], p_ref[4:5], grid)
        acc[...] = jnp.zeros_like(acc)

        def one_group(g, carry):
            local = wz_ref[pl.ds(pl.multiple_of(g * Z_GROUP, Z_GROUP), Z_GROUP)]
            plane = jnp.concatenate(
                [(wy * local[z : z + 1]).astype(BF16) for z in range(Z_GROUP)], axis=0
            )
            acc[...] += dot(f_ref[g], plane, ((1,), (0,)))
            return carry

        lax.fori_loop(low_ref[block], high_ref[block], one_group, 0)
        wx = weights(cells, p_ref[0:1], p_ref[3:4], grid)
        wj = lax.dot_general(
            table_ref[...], wx, (((1,), (0,)), ((), ())),
            precision=lax.Precision.HIGHEST, preferred_element_type=F32,
        )
        product = acc[...].reshape(2, 8, kx, rows) * wj.reshape(2, 1, kx, rows)
        total = jnp.sum(product[0] + product[1], axis=1)
        out_ref[...] = total + earlier[0][...] if earlier else total


def particle_stage(live, low, high, z0, particles, table, fields, chunk, earlier):
    blocks = live.shape[0]
    rows = pl.BlockSpec((8, ROWS), lambda i, *_: (0, i))
    vmem = pl.BlockSpec(memory_space=pltpu.VMEM)
    return pl.pallas_call(
        particle_kernel,
        grid_spec=pltpu.PrefetchScalarGridSpec(
            num_scalar_prefetch=4,
            grid=(blocks,),
            in_specs=[rows, vmem, vmem] + [rows] * len(earlier),
            out_specs=rows,
            scratch_shapes=[
                pltpu.VMEM((fields.shape[1], ROWS), F32),
                pltpu.VMEM((fields.shape[0] * Z_GROUP, ROWS), F32),
            ],
        ),
        out_shape=jax.ShapeDtypeStruct((8, blocks * ROWS), F32),
        compiler_params=pltpu.CompilerParams(vmem_limit_bytes=VMEM_BYTES),
        cost_estimate=cost(
            blocks * ROWS * fields.size, 2 * fields.size + 64 * blocks * ROWS
        ),
        name=f"particle_stage_{chunk}",
    )(live, low, high, z0, particles, table, fields, *earlier)


def per_device(
    source_hat, particle_start, particle_offset, ghost_start, ghost_offset, ghost_slot, counts
):
    _, _, kx, ky, grid = source_hat.shape
    n_gx = lax.axis_size("gx")
    n_gy = lax.axis_size("gy")
    a = lax.axis_index("gx")
    b = lax.axis_index("gy")
    ratio = n_gx // n_gy
    z_count = grid // n_gy
    brick_z = grid // n_gx
    own = particle_start.shape[1]
    ghost = ghost_start.shape[2]
    modes = jnp.asarray(signed(grid), F32)
    mode_x = lax.dynamic_slice(modes, (a * kx,), (kx,))
    mode_y = lax.dynamic_slice(modes, (b * ky,), (ky,))

    mine = jnp.concatenate(
        [
            jnp.concatenate([particle_start.astype(F32), ghost_start[:, 1].astype(F32)], axis=1),
            jnp.concatenate([particle_offset, ghost_offset[:, 1]], axis=1),
            jnp.concatenate([jnp.zeros((1, own), F32), ghost_slot[1:2].astype(F32)], axis=1),
            jnp.concatenate([counts.astype(F32), jnp.zeros((1, own + ghost - 4), F32)], axis=1),
        ]
    )
    every = lax.all_gather(mine, ("gx", "gy")).reshape(n_gx, n_gy, 8, own + ghost)
    near = lax.dynamic_slice(
        every, (ratio * b, 0, 0, 0), (ratio, n_gy, 8, own + ghost)
    ).reshape(ratio * n_gy, 8, own + ghost)
    lists = ratio * n_gy
    particles = jnp.concatenate(
        [
            jnp.moveaxis(near[:, :, :own], 1, 0).reshape(8, lists * own),
            jnp.moveaxis(near[:n_gy, :, own:], 1, 0).reshape(8, n_gy * ghost),
        ],
        axis=1,
    )
    near_counts = near[:, 7, :4].astype(jnp.int32)
    own_live = near_counts[:, :1] - jnp.arange(0, own, ROWS, dtype=jnp.int32)[None]
    ghost_live = near_counts[:n_gy, 2:3] - jnp.arange(0, ghost, ROWS, dtype=jnp.int32)[None]
    live = jnp.concatenate([own_live.reshape(-1), ghost_live.reshape(-1)])
    low, high = [], []
    for which in range(lists):
        first = which // n_gy * brick_z
        last = min(first + brick_z + SUPPORT - 1, z_count)
        low += [first // Z_GROUP] * (own // ROWS)
        high += [-(-last // Z_GROUP)] * (own // ROWS)
    low += [0] * (n_gy * ghost // ROWS)
    high += [-(-(SUPPORT - 1) // Z_GROUP)] * (n_gy * ghost // ROWS)
    low = jnp.asarray(low, jnp.int32)
    high = jnp.asarray(high, jnp.int32)

    index = np.arange(grid)
    angle = (np.outer(index, index) % grid) * (TWO_PI / grid)
    full_table = jnp.asarray(np.stack([np.cos(angle), -np.sin(angle)]), F32)
    z0 = (b * z_count).astype(jnp.int32).reshape(1)
    width = min(MODE_CHUNK, kx)
    chunks = kx // width
    mode_chunks = [mode_x[c * width : (c + 1) * width] for c in range(chunks)]
    sent = [
        z_stage(source_hat, mode_chunks[c], mode_y[:, None], modes[None, :], c, width)
        for c in range(chunks)
    ]

    def interpolated(c, block, earlier):
        block = block.reshape(n_gy, z_count, 5, width, 2 * ky)
        wave_x = jnp.broadcast_to((TWO_PI / grid * mode_chunks[c])[:, None], (width, grid))
        table = lax.dynamic_slice(full_table, (0, a * kx + c * width, 0), (2, width, grid))
        fields = y_stage(block, wave_x, c, earlier)
        return particle_stage(
            live, low, high, z0, particles, table.reshape(2 * width, grid), fields, c, earlier
        )

    earlier = []
    received = None
    for c in range(chunks):
        before = received
        piece = sent[c] if c == 0 else follow(sent[c], before)
        received = lax.all_to_all(piece, "gy", split_axis=0, concat_axis=0, tiled=True)
        if c > 0:
            earlier = [interpolated(c - 1, before, earlier)]
    values = interpolated(chunks - 1, received, earlier)

    own_values = values[:, : lists * own].reshape(8, ratio, n_gy, own)
    ghost_values = ghost_stage(values, particles, own, ghost, n_gy, lists * own)
    spread = jnp.zeros((n_gy, n_gx, 8, own), F32)
    spread = lax.dynamic_update_slice(
        spread, own_values.transpose(2, 1, 0, 3), (0, ratio * b, 0, 0)
    )
    spread = lax.dynamic_update_slice(
        spread,
        ghost_values[:, None],
        (0, (ratio * b + n_gx - 1) % n_gx, 0, 0),
    )
    total = lax.psum_scatter(spread, "gy", scatter_dimension=0, tiled=True)[0]
    total = lax.psum_scatter(total, "gx", scatter_dimension=0, tiled=True)[0]
    return (total[:3], total[3:])


def solution(mesh):
    in_specs = (
        P(None, None, "gx", "gy", None),
        P(None, ("gx", "gy")),
        P(None, ("gx", "gy")),
        P(None, None, ("gx", "gy")),
        P(None, None, ("gx", "gy")),
        P(None, ("gx", "gy")),
        P(("gx", "gy"), None),
    )
    out_specs = (P(None, ("gx", "gy")), P(None, ("gx", "gy")))
    return jax.shard_map(
        per_device, mesh=mesh, in_specs=in_specs, out_specs=out_specs, check_vma=False
    )
```

```python
import functools
import math

import jax
import jax.numpy as jnp
import numpy as np
from jax import lax
from jax.experimental import pallas as pl
from jax.experimental.pallas import tpu as pltpu
from jax.sharding import PartitionSpec as P

SUPPORT = 8
TWO_PI = 2.0 * math.pi
ROWS = 256
Z_GROUP = 8
MODE_CHUNK = 16
VMEM_BYTES = 58 * 1024 * 1024
F32 = jnp.float32
BF16 = jnp.bfloat16


def signed(grid_size):
    index = np.arange(grid_size)
    return np.where(index < grid_size // 2, index, index - grid_size).astype(np.float64)


def dft_tables(grid_size):
    index = np.arange(grid_size)
    angle = (np.outer(index, index) % grid_size) * (TWO_PI / grid_size)
    cosine, sine = np.cos(angle), np.sin(angle)
    plain = np.stack([np.stack([cosine, sine], 1), np.stack([-sine, cosine], 1)])
    wave = (TWO_PI / grid_size * signed(grid_size))[None, :, None, None]
    slope = np.stack([np.stack([-sine, cosine], 1), np.stack([-cosine, -sine], 1)]) * wave
    return plain, slope


def two_parts(table):
    high = table.astype(np.float32).astype(jnp.bfloat16)
    low = (table - high.astype(np.float64)).astype(np.float32).astype(jnp.bfloat16)
    return jnp.asarray(high), jnp.asarray(low)


def split_value(value):
    high = value.astype(BF16)
    return high, (value - high.astype(F32)).astype(BF16)


def exact_dot(left, right_high, right_low):
    high, low = split_value(left)
    dims = ((1,), (0,))
    return dot(high, right_high, dims) + dot(high, right_low, dims) + dot(low, right_high, dims)


def dot(left, right, dims):
    return lax.dot_general(left, right, (dims, ((), ())), preferred_element_type=F32)


def z_kernel(mx_ref, my_ref, mz_ref, s_ref, th_ref, tl_ref, dh_ref, dl_ref, out_ref, xh, xl):
    _, _, jb, ky, grid = s_ref.shape
    first = pl.program_id(0) * jb
    my = my_ref[...]
    mz = mz_ref[...]
    for jj in range(jb):
        mx = mx_ref[first + jj]
        inverse = 1.0 / jnp.maximum(mx * mx + my * my + mz * mz, 1.0)
        for r in range(2):
            s = [s_ref[r, c, jj] for c in range(3)]
            inner = (s[0] * mx + s[1] * my + s[2] * mz) * inverse
            for c, mode in enumerate((mx, my, mz)):
                high, low = split_value(s[c] - mode * inner)
                xh[c, jj * ky : (jj + 1) * ky, r * grid : (r + 1) * grid] = high
                xl[c, jj * ky : (jj + 1) * ky, r * grid : (r + 1) * grid] = low
    for f in range(5):
        c = f if f < 3 else f - 3
        high, low = (th_ref[...], tl_ref[...]) if f < 3 else (dh_ref[...], dl_ref[...])
        dims = ((1,), (1,))
        res = dot(high, xh[c], dims) + dot(low, xh[c], dims) + dot(high, xl[c], dims)
        parts = [
            jnp.concatenate(
                [res[:grid, jj * ky : (jj + 1) * ky], res[grid:, jj * ky : (jj + 1) * ky]], axis=1
            )
            for jj in range(jb)
        ]
        out_ref[:, f] = jnp.swapaxes(jnp.stack(parts), 0, 1)


def cost(flops, nbytes):
    return pl.CostEstimate(flops=flops, bytes_accessed=nbytes, transcendentals=0)


def z_stage(source, mode_x, mode_y, mode_z, chunk, kx):
    _, _, _, ky, grid = source.shape
    jb = 8
    skip = chunk * kx // jb
    plain, slope = dft_tables(grid)

    def arranged(table):
        return two_parts(table.transpose(2, 3, 0, 1).reshape(2 * grid, 2 * grid))

    vmem = pl.BlockSpec(memory_space=pltpu.VMEM)
    return pl.pallas_call(
        z_kernel,
        grid=(kx // jb,),
        in_specs=[
            pl.BlockSpec(memory_space=pltpu.SMEM),
            vmem,
            vmem,
            pl.BlockSpec((2, 3, jb, ky, grid), lambda i: (0, 0, i + skip, 0, 0)),
            vmem,
            vmem,
            vmem,
            vmem,
        ],
        out_specs=pl.BlockSpec((grid, 5, jb, 2 * ky), lambda i: (0, 0, i, 0)),
        out_shape=jax.ShapeDtypeStruct((grid, 5, kx, 2 * ky), F32),
        scratch_shapes=[
            pltpu.VMEM((3, jb * ky, 2 * grid), BF16),
            pltpu.VMEM((3, jb * ky, 2 * grid), BF16),
        ],
        compiler_params=pltpu.CompilerParams(vmem_limit_bytes=VMEM_BYTES),
        cost_estimate=cost(3 * 5 * kx * ky * 8 * grid * grid, 4 * 16 * kx * ky * grid),
        name=f"z_stage_{chunk}",
    )(mode_x, mode_y, mode_z, source, *arranged(plain), *arranged(slope))


def y_kernel(kx_ref, m_ref, th_ref, tl_ref, dh_ref, dl_ref, *rest):
    out_ref = rest[-1]
    pieces, zb, _, kx, width = m_ref.shape
    grid = th_ref.shape[1] // 2
    wave = kx_ref[...]

    def turned(value):
        return jnp.concatenate([-wave * value[:, grid:], wave * value[:, :grid]], axis=1)

    block = jnp.concatenate(
        [m_ref[b].reshape(zb * 5 * kx, width) for b in range(pieces)], axis=1
    )
    components = jnp.concatenate(
        [block[z * 5 * kx : (z * 5 + 3) * kx] for z in range(zb)], axis=0
    )
    y = exact_dot(block, th_ref[...], tl_ref[...])
    d = exact_dot(components, dh_ref[...], dl_ref[...])
    for z in range(zb):
        v = [y[(z * 5 + f) * kx : (z * 5 + f + 1) * kx] for f in range(5)]
        dv = [d[(z * 3 + f) * kx : (z * 3 + f + 1) * kx] for f in range(3)]
        fields = [
            v[0],
            v[1],
            v[2],
            turned(v[0]),
            dv[1],
            0.5 * (dv[0] + turned(v[1])),
            0.5 * (v[3] + turned(v[2])),
            0.5 * (dv[2] + v[4]),
        ]
        both = jnp.concatenate(fields, axis=0).astype(BF16)
        out_ref[0, : 8 * kx, z * grid : (z + 1) * grid] = both[:, :grid]
        out_ref[0, 8 * kx :, z * grid : (z + 1) * grid] = both[:, grid:]


def y_stage(received, wave_x, chunk, after):
    pieces, z_count, _, kx, width = received.shape
    grid = pieces * width // 2
    plain, slope = dft_tables(grid)

    def arranged(table):
        table = table.reshape(2, pieces, width // 2, 2, grid).transpose(1, 0, 2, 3, 4)
        return two_parts(table.reshape(2 * grid, 2 * grid))

    vmem = pl.BlockSpec(memory_space=pltpu.VMEM)
    return pl.pallas_call(
        y_kernel,
        grid=(z_count // Z_GROUP,),
        in_specs=[
            vmem,
            pl.BlockSpec((pieces, Z_GROUP, 5, kx, width), lambda i: (0, i, 0, 0, 0)),
            vmem,
            vmem,
            vmem,
            vmem,
        ]
        + [pl.BlockSpec(memory_space=pl.ANY)] * len(after),
        out_specs=pl.BlockSpec((1, 16 * kx, Z_GROUP * grid), lambda i: (i, 0, 0)),
        out_shape=jax.ShapeDtypeStruct((z_count // Z_GROUP, 16 * kx, Z_GROUP * grid), BF16),
        compiler_params=pltpu.CompilerParams(vmem_limit_bytes=VMEM_BYTES),
        cost_estimate=cost(3 * 8 * 8 * kx * z_count * grid * grid, 72 * kx * z_count * grid),
        name=f"y_stage_{chunk}",
    )(wave_x, received, *arranged(plain), *arranged(slope), *after)


def follow(piece, earlier):
    any_space = pl.BlockSpec(memory_space=pl.ANY)
    return pl.pallas_call(
        lambda *refs: None,
        in_specs=[any_space, any_space],
        out_specs=any_space,
        out_shape=jax.ShapeDtypeStruct(piece.shape, piece.dtype),
        input_output_aliases={0: 0},
        compiler_params=pltpu.CompilerParams(vmem_limit_bytes=VMEM_BYTES),
        name="follow",
    )(piece, earlier)


def ghost_kernel(v_ref, p_ref, out_ref):
    own = out_ref.shape[2]
    ghost = v_ref.shape[1]
    slots = lax.broadcasted_iota(jnp.int32, (own, ghost), 0).astype(F32)
    hit = jnp.where(slots == p_ref[6:7], 1.0, 0.0).astype(BF16)
    value = v_ref[...]
    first, rest = split_value(value)
    rest = value - first.astype(F32)
    second, _ = split_value(rest)
    third = (rest - second.astype(F32)).astype(BF16)
    dims = ((1,), (1,))
    out_ref[0] = dot(first, hit, dims) + dot(second, hit, dims) + dot(third, hit, dims)


def ghost_stage(values, particles, own, ghost, lists, skip):
    block = pl.BlockSpec((8, ghost), lambda i: (0, i + skip // ghost))
    return pl.pallas_call(
        ghost_kernel,
        grid=(lists,),
        in_specs=[block, block],
        out_specs=pl.BlockSpec((1, 8, own), lambda i: (i, 0, 0)),
        out_shape=jax.ShapeDtypeStruct((lists, 8, own), F32),
        compiler_params=pltpu.CompilerParams(vmem_limit_bytes=VMEM_BYTES),
        name="ghost_stage",
    )(values, particles)


def weights(cells, start, offset, grid):
    distance = cells - start
    distance = jnp.where(distance < 0, distance + grid, distance)
    shifted = distance - (SUPPORT // 2 - 1) - offset
    return jnp.where(distance < SUPPORT, jnp.exp(-5.6 * shifted * shifted / SUPPORT), 0.0)


def particle_kernel(
    live_ref, low_ref, high_ref, z0_ref, p_ref, table_ref, f_ref, *rest
):
    *earlier, out_ref, acc, wz_ref = rest
    block = pl.program_id(0)
    grid = table_ref.shape[1]
    groups = f_ref.shape[0]
    kx = table_ref.shape[0] // 2
    rows = p_ref.shape[1]
    live = live_ref[block]

    @pl.when(live <= 0)
    def _():
        out_ref[...] = jnp.zeros_like(out_ref)

    @pl.when(live > 0)
    def _():
        cells = lax.broadcasted_iota(jnp.int32, (grid, rows), 0).astype(F32)
        z_cells = lax.broadcasted_iota(jnp.int32, (groups * Z_GROUP, rows), 0) + z0_ref[0]
        wz = weights(z_cells.astype(F32), p_ref[2:3], p_ref[5:6], grid)
        lane = lax.broadcasted_iota(jnp.int32, (groups * Z_GROUP, rows), 1)
        wz_ref[...] = jnp.where(lane < live, wz, 0.0)
        wy = weights(cells, p_ref[1:2], p_ref[4:5], grid)
        acc[...] = jnp.zeros_like(acc)

        def one_group(g, carry):
            local = wz_ref[pl.ds(pl.multiple_of(g * Z_GROUP, Z_GROUP), Z_GROUP)]
            plane = jnp.concatenate(
                [(wy * local[z : z + 1]).astype(BF16) for z in range(Z_GROUP)], axis=0
            )
            acc[...] += dot(f_ref[g], plane, ((1,), (0,)))
            return carry

        lax.fori_loop(low_ref[block], high_ref[block], one_group, 0)
        wx = weights(cells, p_ref[0:1], p_ref[3:4], grid)
        wj = lax.dot_general(
            table_ref[...], wx, (((1,), (0,)), ((), ())),
            precision=lax.Precision.HIGHEST, preferred_element_type=F32,
        )
        product = acc[...].reshape(2, 8, kx, rows) * wj.reshape(2, 1, kx, rows)
        total = jnp.sum(product[0] + product[1], axis=1)
        out_ref[...] = total + earlier[0][...] if earlier else total


def particle_stage(live, low, high, z0, particles, table, fields, chunk, earlier):
    blocks = live.shape[0]
    rows = pl.BlockSpec((8, ROWS), lambda i, *_: (0, i))
    vmem = pl.BlockSpec(memory_space=pltpu.VMEM)
    return pl.pallas_call(
        particle_kernel,
        grid_spec=pltpu.PrefetchScalarGridSpec(
            num_scalar_prefetch=4,
            grid=(blocks,),
            in_specs=[rows, vmem, vmem] + [rows] * len(earlier),
            out_specs=rows,
            scratch_shapes=[
                pltpu.VMEM((fields.shape[1], ROWS), F32),
                pltpu.VMEM((fields.shape[0] * Z_GROUP, ROWS), F32),
            ],
        ),
        out_shape=jax.ShapeDtypeStruct((8, blocks * ROWS), F32),
        compiler_params=pltpu.CompilerParams(vmem_limit_bytes=VMEM_BYTES),
        cost_estimate=cost(
            blocks * ROWS * fields.size, 2 * fields.size + 64 * blocks * ROWS
        ),
        name=f"particle_stage_{chunk}",
    )(live, low, high, z0, particles, table, fields, *earlier)


def per_device(
    source_hat, particle_start, particle_offset, ghost_start, ghost_offset, ghost_slot, counts
):
    _, _, kx, ky, grid = source_hat.shape
    n_gx = lax.axis_size("gx")
    n_gy = lax.axis_size("gy")
    a = lax.axis_index("gx")
    b = lax.axis_index("gy")
    ratio = n_gx // n_gy
    z_count = grid // n_gy
    brick_z = grid // n_gx
    own = particle_start.shape[1]
    ghost = ghost_start.shape[2]
    modes = jnp.asarray(signed(grid), F32)
    mode_x = lax.dynamic_slice(modes, (a * kx,), (kx,))
    mode_y = lax.dynamic_slice(modes, (b * ky,), (ky,))

    mine = jnp.concatenate(
        [
            jnp.concatenate([particle_start.astype(F32), ghost_start[:, 1].astype(F32)], axis=1),
            jnp.concatenate([particle_offset, ghost_offset[:, 1]], axis=1),
            jnp.concatenate([jnp.zeros((1, own), F32), ghost_slot[1:2].astype(F32)], axis=1),
            jnp.concatenate([counts.astype(F32), jnp.zeros((1, own + ghost - 4), F32)], axis=1),
        ]
    )
    every = lax.all_gather(mine, ("gx", "gy")).reshape(n_gx, n_gy, 8, own + ghost)
    near = lax.dynamic_slice(
        every, (ratio * b, 0, 0, 0), (ratio, n_gy, 8, own + ghost)
    ).reshape(ratio * n_gy, 8, own + ghost)
    lists = ratio * n_gy
    particles = jnp.concatenate(
        [
            jnp.moveaxis(near[:, :, :own], 1, 0).reshape(8, lists * own),
            jnp.moveaxis(near[:n_gy, :, own:], 1, 0).reshape(8, n_gy * ghost),
        ],
        axis=1,
    )
    near_counts = near[:, 7, :4].astype(jnp.int32)
    own_live = near_counts[:, :1] - jnp.arange(0, own, ROWS, dtype=jnp.int32)[None]
    ghost_live = near_counts[:n_gy, 2:3] - jnp.arange(0, ghost, ROWS, dtype=jnp.int32)[None]
    live = jnp.concatenate([own_live.reshape(-1), ghost_live.reshape(-1)])
    low, high = [], []
    for which in range(lists):
        first = which // n_gy * brick_z
        last = min(first + brick_z + SUPPORT - 1, z_count)
        low += [first // Z_GROUP] * (own // ROWS)
        high += [-(-last // Z_GROUP)] * (own // ROWS)
    low += [0] * (n_gy * ghost // ROWS)
    high += [-(-(SUPPORT - 1) // Z_GROUP)] * (n_gy * ghost // ROWS)
    low = jnp.asarray(low, jnp.int32)
    high = jnp.asarray(high, jnp.int32)

    index = np.arange(grid)
    angle = (np.outer(index, index) % grid) * (TWO_PI / grid)
    full_table = jnp.asarray(np.stack([np.cos(angle), -np.sin(angle)]), F32)
    z0 = (b * z_count).astype(jnp.int32).reshape(1)
    width = min(MODE_CHUNK, kx)
    chunks = kx // width
    mode_chunks = [mode_x[c * width : (c + 1) * width] for c in range(chunks)]
    sent = [
        z_stage(source_hat, mode_chunks[c], mode_y[:, None], modes[None, :], c, width)
        for c in range(chunks)
    ]

    def interpolated(c, block, earlier):
        block = block.reshape(n_gy, z_count, 5, width, 2 * ky)
        wave_x = jnp.broadcast_to((TWO_PI / grid * mode_chunks[c])[:, None], (width, grid))
        table = lax.dynamic_slice(full_table, (0, a * kx + c * width, 0), (2, width, grid))
        fields = y_stage(block, wave_x, c, earlier)
        return particle_stage(
            live, low, high, z0, particles, table.reshape(2 * width, grid), fields, c, earlier
        )

    earlier = []
    received = None
    for c in range(chunks):
        before = received
        piece = sent[c] if c == 0 else follow(sent[c], before)
        received = lax.all_to_all(piece, "gy", split_axis=0, concat_axis=0, tiled=True)
        if c > 0:
            earlier = [interpolated(c - 1, before, earlier)]
    values = interpolated(chunks - 1, received, earlier)

    own_values = values[:, : lists * own].reshape(8, ratio, n_gy, own)
    ghost_values = ghost_stage(values, particles, own, ghost, n_gy, lists * own)
    pieces = jnp.concatenate(
        [own_values.transpose(2, 1, 0, 3), ghost_values[:, None]], axis=1
    )
    pieces = lax.all_to_all(pieces, "gy", split_axis=0, concat_axis=0, tiled=True)
    ghost_part = jnp.roll(pieces[:, ratio], -1, axis=0)
    sums = jnp.concatenate(
        [pieces[:, : ratio - 1], (pieces[:, ratio - 1] + ghost_part)[:, None]], axis=1
    ).reshape(n_gx, 8, own)
    total = lax.psum_scatter(sums, "gx", scatter_dimension=0, tiled=True)[0]
    return (total[:3], total[3:])


def solution(mesh):
    in_specs = (
        P(None, None, "gx", "gy", None),
        P(None, ("gx", "gy")),
        P(None, ("gx", "gy")),
        P(None, None, ("gx", "gy")),
        P(None, None, ("gx", "gy")),
        P(None, ("gx", "gy")),
        P(("gx", "gy"), None),
    )
    out_specs = (P(None, ("gx", "gy")), P(None, ("gx", "gy")))
    return jax.shard_map(
        per_device, mesh=mesh, in_specs=in_specs, out_specs=out_specs, check_vma=False
    )
```
